256 devices in a mesh: tok: 8 (over z_hi, core), win: 4 (over y), wout: 8 (over z_lo, x).
Axes of the slice: x: 4, y: 4, z: 8 (z_hi: 4, z_lo: 2; z = z_hi * 2 + z_lo), core: 2. Of those that a mesh axis runs over, the one named last changes fastest.
Arguments:
- acts: bfloat16 [1024, 8192], P(('tok', 'wout'), 'win'), may hold values from -6 to 6
- gate_weight: bfloat16 [29568, 8192], P(('tok', 'wout'), 'win'), may hold values from -0.0625 to 0.0625
- up_weight: bfloat16 [29568, 8192], P(('tok', 'wout'), 'win'), may hold values from -0.0625 to 0.0625
- hidden_grad: bfloat16 [1024, 29568], P('wout', 'tok'), may hold values from -2 to 2
Outputs:
- input_grad: bfloat16 [1024, 8192], P(('tok', 'wout'), 'win')
- gate_weight_grad: bfloat16 [29568, 8192], P(('tok', 'wout'), 'win')
- up_weight_grad: bfloat16 [29568, 8192], P(('tok', 'wout'), 'win')
The draws below stay inside these ranges and needn't reach their ends.
All inputs are finite; a program needn't handle non-finite values.
Results may differ from the reference program's by a relative error of at most 0.0049.
Values may be sent and summed in bfloat16 or wider, within the bound.
No kernel may reach another device: no remote copies, remote signals or barrier semaphores. Data moves between devices by JAX's collectives and lax.ppermute only.
A program may use at most 192 MiB of HBM per device.

```python
import jax
import jax.numpy as jnp

D = 8192
FF = 29568
TOKENS = 1024


def strengthened(drawn, key, source, target, blocks, factor):
    def block_of(dim):
        return (jnp.arange(drawn.shape[dim]) // (drawn.shape[dim] // blocks)).reshape((-1,) + (1,) * (drawn.ndim - 1 - dim))

    one_side = jax.random.permutation(key, blocks)[block_of(target)]
    far = (block_of(target) + blocks // 2) % blocks
    return jnp.where((block_of(source) == one_side) | (block_of(source) == far), factor * drawn, drawn)


def shard_levels(own_key, shape, split, low, largest):
    level, own = 1.0, jax.random.fold_in(own_key, 6)
    for position, shards_of in split:
        steps = jnp.exp(jax.random.uniform(jax.random.fold_in(own, position), (shards_of,), jnp.float32, low / len(split), largest / len(split)))
        level = level * jnp.repeat(steps, shape[position] // shards_of).reshape([-1 if axis == position else 1 for axis in range(len(shape))])
    return level


def scatter_about(own_key, extent, spread, most, shards=(), held_as=jnp.bfloat16):
    drawn = spread * jax.random.normal(own_key, extent, jnp.float32)
    if shards:
        drawn = drawn * shard_levels(own_key, extent, shards, -0.22, 0.18)
    return jnp.clip(drawn, -most, most).astype(held_as)


def bell_draw_with(own_key, extent, width, limit, shards, heavy, held_as=jnp.bfloat16):
    drawn = width * jax.random.normal(own_key, extent, jnp.float32)
    if shards:
        drawn = drawn * shard_levels(own_key, extent, shards, -0.22, 0.18)
    return jnp.clip(strengthened(drawn, jax.random.fold_in(own_key, 3), *heavy), -limit, limit).astype(held_as)


def setup_inputs(seed: int = 0) -> dict:
    keys = jax.random.split(jax.random.key(seed), 5)
    return {
        "acts": scatter_about(keys[0], (TOKENS, D), 1.0, 6.0, ((0, 64), (1, 4))),
        "gate_weight": scatter_about(keys[1], (FF, D), D ** -0.5, 0.0625, ((0, 64), (1, 4))),
        "up_weight": scatter_about(keys[2], (FF, D), D ** -0.5, 0.0625, ((0, 64), (1, 4))),
        "hidden_grad": bell_draw_with(keys[3], (TOKENS, FF), 0.25, 2.0, ((0, 8), (1, 8)), (1, 0, 8, 2.0)),
    }


def swiglu_grads(gate_pre, up_pre, grad_f32):
    gate_sig = jax.nn.sigmoid(gate_pre)
    gate_grad = (grad_f32 * up_pre * gate_sig * (1.0 + gate_pre * (1.0 - gate_sig))).astype(jnp.bfloat16)
    up_grad = (grad_f32 * gate_pre * gate_sig).astype(jnp.bfloat16)
    return gate_grad, up_grad


def reference(acts, gate_weight, up_weight, hidden_grad):
    gate_pre = jnp.dot(acts, gate_weight.T, preferred_element_type=jnp.float32)
    up_pre = jnp.dot(acts, up_weight.T, preferred_element_type=jnp.float32)
    gate_grad, up_grad = swiglu_grads(gate_pre, up_pre, hidden_grad.astype(jnp.float32))
    input_grad = jnp.dot(gate_grad, gate_weight, preferred_element_type=jnp.float32) + jnp.dot(up_grad, up_weight, preferred_element_type=jnp.float32)
    gate_weight_grad = jnp.dot(gate_grad.T, acts, preferred_element_type=jnp.float32)
    up_weight_grad = jnp.dot(up_grad.T, acts, preferred_element_type=jnp.float32)
    return input_grad.astype(jnp.bfloat16), gate_weight_grad.astype(jnp.bfloat16), up_weight_grad.astype(jnp.bfloat16)
```

```python
import jax
import jax.numpy as jnp
import numpy as np
from jax import lax
from jax.sharding import Mesh, PartitionSpec as P

F32 = jnp.float32
BF16 = jnp.bfloat16
NX, NY, ZH, ZL, NC = 4, 4, 4, 2, 2


def shift(value, axis, by, size):
    return lax.ppermute(value, axis, [(i, (i + by) % size) for i in range(size)])


def x_shift(value, by):
    return shift(value, "x", by, NX)


def y_shift(value, by):
    return shift(value, "y", by, NY)


def core_swap(value):
    return shift(value, "c", 1, NC)


def rolled(value, by, axis):
    size = value.shape[axis]
    twice = jnp.concatenate([value, value], axis=axis)
    return lax.dynamic_slice_in_dim(twice, by, size, axis)


def dot_nt(a, b):
    return lax.dot_general(a, b, (((1,), (1,)), ((), ())), preferred_element_type=F32)


def dot_tn(a, b):
    return lax.dot_general(a, b, (((0,), (0,)), ((), ())), preferred_element_type=F32)


def swiglu_grads(gate_pre, up_pre, grad):
    gate_sig = jax.nn.sigmoid(gate_pre)
    gate_grad = grad * up_pre * gate_sig * (1.0 + gate_pre * (1.0 - gate_sig))
    up_grad = grad * gate_pre * gate_sig
    return gate_grad, up_grad


def local(acts, gate_weight, up_weight, hidden_grad):
    rows, width = acts.shape
    units = gate_weight.shape[0]
    half = rows // 2
    x, y, c = lax.axis_index("x"), lax.axis_index("y"), lax.axis_index("c")
    weights = jnp.concatenate([gate_weight, up_weight], axis=0)

    mine = lax.all_to_all(
        jnp.broadcast_to(acts[None], (ZL * ZH, rows, width)), ("zl", "zh"), split_axis=0, concat_axis=0, tiled=True
    )
    mine = mine.reshape(ZL, ZH, 2, half, width).transpose(0, 2, 1, 3, 4).reshape(NY, ZH * half, width)
    mine = rolled(mine, y, 0)
    per = ZH * half

    cot = hidden_grad.reshape(ZL, NX, 2, half, ZL * NX, units)
    cot = lax.dynamic_index_in_dim(cot, y // 2, 0, keepdims=False)
    cot = lax.dynamic_index_in_dim(cot, y % 2, 1, keepdims=False)
    cot = cot.transpose(2, 0, 1, 3)
    cot = lax.all_to_all(cot, ("zl", "x"), split_axis=0, concat_axis=0, tiled=True)
    cot = cot.reshape(ZH, NC, NX, half, units).transpose(2, 1, 0, 3, 4).reshape(NX, NC, per, units)
    cot = rolled(rolled(cot, x, 0), c, 1)

    right = x_shift(mine, -1)
    left = x_shift(mine, 1)
    far_a = x_shift(right[: NY // 2], -1)
    far_b = x_shift(left[NY // 2 :], 1)
    far = jnp.concatenate([far_a, far_b], axis=0)

    def with_other(blocks):
        other = core_swap(blocks)
        return jnp.concatenate([blocks, other], axis=1)

    def chunk_of(owners):
        parts = [with_other(o) for o in owners]
        return jnp.concatenate(parts, axis=1)

    chunks = [chunk_of([mine]), chunk_of([right, left]), chunk_of([far])]
    owners = [[0], [1, 3], [2]]

    def forward(chunk, owner):
        n = chunk.shape[1]
        pre = dot_nt(chunk.reshape(NY * n, width), weights).reshape(NY, n, 2 * units)
        sent = pre.astype(BF16)
        total = pre[0]
        for s in (2, 1, 3):
            total = total + y_shift(sent[s], s).astype(F32)
        grad = jnp.concatenate([cot[o].reshape(NC * per, units) for o in owner], axis=0).astype(F32)
        gate_grad, up_grad = swiglu_grads(total[:, :units], total[:, units:], grad)
        return jnp.concatenate([gate_grad, up_grad], axis=1).astype(BF16)

    own_grads = [forward(ch, ow) for ch, ow in zip(chunks, owners)]

    grads = [None] * 3
    partial = [None] * NX
    for i in (1, 2, 0):
        g = own_grads[i]
        n = g.shape[0]
        got = {s: y_shift(g, s) for s in (2, 1, 3)}
        full = jnp.concatenate([g[None], got[3][None], got[2][None], got[1][None]], axis=0)
        grads[i] = full
        back = jnp.dot(full.reshape(NY * n, 2 * units), weights, preferred_element_type=F32)
        back = back.reshape(NY, len(owners[i]), NC, per, width)
        for k, o in enumerate(owners[i]):
            kept = back[:, k, 0]
            kept = kept + core_swap(back[:, k, 1].astype(BF16)).astype(F32)
            partial[o] = kept
    total = partial[0]
    for o in (1, 3, 2):
        total = total + x_shift(partial[o].astype(BF16), o).astype(F32)

    total = rolled(total.astype(BF16), (NY - y) % NY, 0)
    total = total.reshape(ZL, 2, ZH, half, width).transpose(0, 2, 1, 3, 4).reshape(ZL * ZH, rows, width)
    got = lax.all_to_all(total, ("zl", "zh"), split_axis=0, concat_axis=0, tiled=True)
    input_grad = got.astype(F32).sum(axis=0).astype(BF16)

    all_tokens = jnp.concatenate([ch.reshape(-1, width) for ch in chunks], axis=0)
    all_grads = jnp.concatenate([g.reshape(-1, 2 * units) for g in grads], axis=0)
    gate_weight_grad = dot_tn(all_grads[:, :units], all_tokens).astype(BF16)
    up_weight_grad = dot_tn(all_grads[:, units:], all_tokens).astype(BF16)
    return input_grad, gate_weight_grad, up_weight_grad


def solution(mesh):
    fine = Mesh(np.asarray(mesh.devices).reshape(ZH, NC, NY, ZL, NX), ("zh", "c", "y", "zl", "x"))
    rows = ("zh", "c", "zl", "x")
    in_specs = (P(rows, "y"), P(rows, "y"), P(rows, "y"), P(("zl", "x"), ("zh", "c")))
    out_specs = (P(rows, "y"), P(rows, "y"), P(rows, "y"))
    return jax.shard_map(local, mesh=fine, in_specs=in_specs, out_specs=out_specs, check_vma=False)
```

```python
import functools

import jax
import jax.numpy as jnp
import numpy as np
from jax import lax
from jax.experimental import pallas as pl
from jax.experimental.pallas import tpu as pltpu
from jax.sharding import Mesh, PartitionSpec as P

F32 = jnp.float32
BF16 = jnp.bfloat16
NX, NY, ZH, ZL, NC = 4, 4, 4, 2, 2
OWNED = 16
BLOCK = ZL * ZH * OWNED
PART = ZH * OWNED


def cost(microseconds):
    return pl.CostEstimate(flops=int(1.1e9 * microseconds), bytes_accessed=1, transcendentals=0)


VMEM = pl.BlockSpec(memory_space=pltpu.VMEM)
SMEM = pl.BlockSpec(memory_space=pltpu.SMEM)
PARAMS = pltpu.CompilerParams(vmem_limit_bytes=16 * 2**20)


def shift(value, axis, by, size):
    return lax.ppermute(value, axis, [(i, (i + by) % size) for i in range(size)])


def x_shift(value, by):
    return shift(value, "x", by, NX)


def y_shift(value, by):
    return shift(value, "y", by, NY)


def core_swap(value):
    return shift(value, "c", 1, NC)


def exchange(value, axes):
    return lax.all_to_all(value, axes, split_axis=0, concat_axis=0, tiled=True)


def rolled(value, by, axis):
    size = value.shape[axis]
    twice = jnp.concatenate([value, value], axis=axis)
    return lax.dynamic_slice_in_dim(twice, by, size, axis)


def after(value, *others):
    return lax.optimization_barrier((value,) + others)[0]


def offset(x, owner):
    return lax.rem(owner - x + 2 * NX, NX)


def part_of(ref, half):
    return ref[...] if ref.shape[0] == PART else ref[half * PART : (half + 1) * PART]


def forward_kernel(half, at_ref, *refs):
    blocks, weights, tokens, outs, pre = refs[:NX], refs[NX : NX + 4], refs[NX + 4], refs[NX + 5 : -1], refs[-1]
    x, y = at_ref[0], at_ref[1]
    for o, block in enumerate(blocks):
        tokens[o * PART : (o + 1) * PART] = part_of(block, half)
    for side, weight in enumerate(weights):
        value = lax.dot_general(tokens[...], weight[...], (((1,), (1,)), ((), ())), preferred_element_type=F32)
        for o in range(NX):
            pre[o] = value[o * PART : (o + 1) * PART]
        for s, out in enumerate(outs):
            out[side] = pre[offset(x, y + s)].astype(out.dtype)


def forward(at, half, blocks, weights):
    units, width = weights[0].shape
    part = jax.ShapeDtypeStruct((4, PART, units), BF16)
    return pl.pallas_call(
        functools.partial(forward_kernel, half),
        out_shape=(
            jax.ShapeDtypeStruct((NX * PART, width), BF16),
            jax.ShapeDtypeStruct((4, PART, units), F32),
            part,
            part,
            part,
        ),
        in_specs=[SMEM] + [VMEM] * 8,
        out_specs=(VMEM,) * 5,
        scratch_shapes=[pltpu.VMEM((NX, PART, units), F32)],
        compiler_params=PARAMS,
        cost_estimate=cost(0.1),
        name="forward%d" % half,
    )(at, *blocks, *weights)


def gradient_kernel(half, at_ref, own, from1, from2, from3, cot, cot_sibling, out, grad):
    x, c, zl = at_ref[0], at_ref[2], at_ref[3]
    for k, cotangent in enumerate((cot, cot_sibling)):
        for z in range(ZH):
            x_from = lax.rem(x - (z % 2) * NC - c + NX, NX)
            zl_from = lax.rem(zl + z // 2, ZL)
            grad[z * OWNED : (z + 1) * OWNED, :] = cotangent[x_from, zl_from, pl.ds(half * OWNED, OWNED), :]

        def total(side):
            near = own[side] + from1[side].astype(F32)
            return near + (from2[side].astype(F32) + from3[side].astype(F32))

        gate_pre, up_pre = total(2 * k), total(2 * k + 1)
        gate_sig = jax.nn.sigmoid(gate_pre)
        scaled = grad[...].astype(F32) * gate_sig
        out[2 * k] = (scaled * up_pre * (1.0 + gate_pre * (1.0 - gate_sig))).astype(BF16)
        out[2 * k + 1] = (scaled * gate_pre).astype(BF16)


def gradient(at, half, own, received, cot, cot_sibling):
    return pl.pallas_call(
        functools.partial(gradient_kernel, half),
        out_shape=jax.ShapeDtypeStruct(own.shape, BF16),
        in_specs=[SMEM] + [VMEM] * 6,
        out_specs=VMEM,
        scratch_shapes=[pltpu.VMEM(own.shape[1:], BF16)],
        compiler_params=PARAMS,
        cost_estimate=cost(0.1 + 6 * half),
        name="gradient%d" % half,
    )(at, own, *received, cot, cot_sibling)


def backward_kernel(tile, at_ref, own, from1, from2, from3, *refs):
    weights, fulls, outs = refs[:4], refs[4:6], refs[6:]
    x, y = at_ref[0], at_ref[1]
    for side in range(4):
        for s, ref in enumerate((own, from1, from2, from3)):
            fulls[side // 2][side % 2, offset(x, y - s)] = ref[side]
    rows = [fulls[side // 2][side % 2].reshape(NX * PART, own.shape[2]) for side in range(4)]
    for col in range(0, outs[0].shape[1], tile):
        total = None
        for side, weight in enumerate(weights):
            term = jnp.dot(rows[side], weight[:, col : col + tile], preferred_element_type=F32)
            total = term if total is None else total + term
        for o, out in enumerate(outs):
            out[:, col : col + tile] = total[o * PART : (o + 1) * PART].astype(out.dtype)


def backward(at, half, pieces, weights):
    units, width = weights[0].shape
    part = jax.ShapeDtypeStruct((PART, width), BF16)
    full = jax.ShapeDtypeStruct((2, NX, PART, units), BF16)
    return pl.pallas_call(
        functools.partial(backward_kernel, min(512, width)),
        out_shape=(
            full,
            full,
            jax.ShapeDtypeStruct((PART, width), F32),
            part,
            part,
            part,
        ),
        in_specs=[SMEM] + [VMEM] * 8,
        out_specs=(VMEM,) * 6,
        compiler_params=PARAMS,
        cost_estimate=cost(5),
        name="backward%d" % half,
    )(at, *pieces, *weights)


def weights_kernel(side, tile, *refs):
    n = len(refs) // 2
    tokens, fulls, out = refs[:n], refs[n : 2 * n], refs[-1]
    rows = jnp.concatenate([f[side].reshape(NX * PART, out.shape[0]) for f in fulls], axis=0)
    for col in range(0, out.shape[1], tile):
        total = lax.dot_general(
            rows,
            jnp.concatenate([r[:, col : col + tile] for r in tokens], axis=0),
            (((0,), (0,)), ((), ())),
            preferred_element_type=F32,
        )
        out[:, col : col + tile] = total.astype(BF16)


def weight_grad(tokens, fulls, side):
    width = tokens[0].shape[1]
    return pl.pallas_call(
        functools.partial(weights_kernel, side, min(512, width)),
        out_shape=jax.ShapeDtypeStruct((fulls[0].shape[3], width), BF16),
        in_specs=[VMEM] * (2 * len(tokens)),
        out_specs=VMEM,
        compiler_params=PARAMS,
        cost_estimate=cost(5),
        name="weight_grad%d" % side,
    )(*tokens, *fulls)


def halves_kernel(a, b, a_out, b_out):
    a_out[...] = a[: a_out.shape[0]]
    b_out[...] = b[b_out.shape[0] :]


def halves(a, b):
    rows, width = a.shape
    out = jax.ShapeDtypeStruct((rows // 2, width), a.dtype)
    return pl.pallas_call(
        halves_kernel,
        out_shape=(out, out),
        in_specs=[VMEM] * 2,
        out_specs=(VMEM, VMEM),
        compiler_params=PARAMS,
        cost_estimate=cost(0.1),
        name="halves",
    )(a, b)


def local(acts, gate_weight, up_weight, hidden_grad):
    rows, width = acts.shape
    units = gate_weight.shape[0]
    x, y, c, zl = lax.axis_index("x"), lax.axis_index("y"), lax.axis_index("c"), lax.axis_index("zl")
    at = jnp.stack([x, y, c, zl]).astype(jnp.int32)

    weights = [gate_weight, up_weight, core_swap(gate_weight), core_swap(up_weight)]

    cot = hidden_grad.reshape(ZL, NX, OWNED, ZL, NX, units)
    cot = lax.dynamic_index_in_dim(cot, y, 1, keepdims=False).reshape(ZL * OWNED, ZL, NX, units)
    cot = rolled(rolled(cot.transpose(1, 2, 0, 3), zl, 0), x, 1)

    mine = exchange(jnp.broadcast_to(acts[None], (ZL * ZH, rows, width)), ("zl", "zh")).reshape(BLOCK, width)
    mine, cot, *weights = lax.optimization_barrier((mine, cot, *weights))
    right = x_shift(mine, -1)
    left = x_shift(mine, 1)

    passed = shift(cot[1], "zl", 1, ZL)
    cot = [jnp.stack([cot[0, s], passed[s]]) for s in range(NX)]
    cot = jnp.stack([cot[0]] + [x_shift(cot[s], s) for s in range(1, NX)])

    right_half, left_half = halves(right, left)
    far = lax.optimization_barrier((x_shift(right_half, -1), x_shift(left_half, 1)))
    chunks = [[mine, right, f, left] for f in far]

    tokens0, own0, *sent0 = forward(after(at, cot), 0, chunks[0], weights)
    got0 = [y_shift(t, s) for s, t in enumerate(sent0, 1)]
    tokens1, own1, *sent1 = forward(after(at, own0), 1, chunks[1], weights)
    got0, own1 = lax.optimization_barrier((got0, own1))
    got1 = [y_shift(t, s) for s, t in enumerate(sent1, 1)]
    cot_sibling = core_swap(after(cot, own1))
    grad0 = gradient(at, 0, own0, got0, cot, cot_sibling)
    pieces0 = [grad0] + [y_shift(grad0, s) for s in (1, 2, 3)]
    grad1 = gradient(after(at, grad0), 1, own1, got1, cot, cot_sibling)
    pieces1 = [grad1] + [y_shift(grad1, s) for s in (1, 2, 3)]

    full0, passed0, kept0, *parts0 = backward(after(at, grad1), 0, pieces0, weights)
    sums0 = [x_shift(part, o) for o, part in enumerate(parts0, 1)]
    full1, passed1, kept1, *parts1 = backward(after(at, kept0), 1, pieces1, weights)
    parts1, sums0 = lax.optimization_barrier((parts1, sums0))
    sums1 = [x_shift(part, o) for o, part in enumerate(parts1, 1)]

    totals = []
    for kept, sums in ((kept0, sums0), (kept1, sums1)):
        for part in sums:
            kept = kept + part.astype(F32)
        totals.append(kept.astype(BF16))
    total = jnp.concatenate(totals, axis=0)
    got = exchange(total.reshape(ZL * ZH, rows, width), ("zl", "zh"))
    tokens = [tokens0, tokens1, core_swap(tokens0), core_swap(tokens1)]
    fulls = [full0, full1, core_swap(passed0), core_swap(passed1)]
    gate_weight_grad, up_weight_grad = [weight_grad(tokens, fulls, side) for side in (0, 1)]
    got, gate_weight_grad, up_weight_grad = lax.optimization_barrier((got, gate_weight_grad, up_weight_grad))
    input_grad = got.astype(F32).sum(axis=0).astype(BF16)
    return input_grad, gate_weight_grad, up_weight_grad


def solution(mesh):
    fine = Mesh(np.asarray(mesh.devices).reshape(ZH, NC, NY, ZL, NX), ("zh", "c", "y", "zl", "x"))
    rows = ("zh", "c", "zl", "x")
    in_specs = (P(rows, "y"), P(rows, "y"), P(rows, "y"), P(("zl", "x"), ("zh", "c")))
    out_specs = (P(rows, "y"), P(rows, "y"), P(rows, "y"))
    return jax.shard_map(local, mesh=fine, in_specs=in_specs, out_specs=out_specs, check_vma=False)
```

```python
import functools

import jax
import jax.numpy as jnp
import numpy as np
from jax import lax
from jax.experimental import pallas as pl
from jax.experimental.pallas import tpu as pltpu
from jax.sharding import Mesh, PartitionSpec as P

F32 = jnp.float32
BF16 = jnp.bfloat16
NX, NY, ZH, ZL, NC = 4, 4, 4, 2, 2
OWNED = 16
BLOCK = ZL * ZH * OWNED
PART = ZH * OWNED


def cost(microseconds):
    return pl.CostEstimate(flops=int(1.1e9 * microseconds), bytes_accessed=1, transcendentals=0)


VMEM = pl.BlockSpec(memory_space=pltpu.VMEM)
SMEM = pl.BlockSpec(memory_space=pltpu.SMEM)
PARAMS = pltpu.CompilerParams(vmem_limit_bytes=16 * 2**20)


def shift(value, axis, by, size):
    return lax.ppermute(value, axis, [(i, (i + by) % size) for i in range(size)])


def x_shift(value, by):
    return shift(value, "x", by, NX)


def y_shift(value, by):
    return shift(value, "y", by, NY)


def core_swap(value):
    return shift(value, "c", 1, NC)


def exchange(value, axes):
    return lax.all_to_all(value, axes, split_axis=0, concat_axis=0, tiled=True)


def rolled(value, by, axis):
    size = value.shape[axis]
    twice = jnp.concatenate([value, value], axis=axis)
    return lax.dynamic_slice_in_dim(twice, by, size, axis)


def after(value, *others):
    return lax.optimization_barrier((value,) + others)[0]


def offset(x, owner):
    return lax.rem(owner - x + 2 * NX, NX)


def part_of(ref, half):
    return ref[...] if ref.shape[0] == PART else ref[half * PART : (half + 1) * PART]


def forward_kernel(half, at_ref, *refs):
    blocks, weights, tokens, outs, pre = refs[:NX], refs[NX : NX + 4], refs[NX + 4], refs[NX + 5 : -1], refs[-1]
    x, y = at_ref[0], at_ref[1]
    for o, block in enumerate(blocks):
        tokens[o * PART : (o + 1) * PART] = part_of(block, half)
    for side, weight in enumerate(weights):
        value = lax.dot_general(tokens[...], weight[...], (((1,), (1,)), ((), ())), preferred_element_type=F32)
        for o in range(NX):
            pre[o] = value[o * PART : (o + 1) * PART]
        for s, out in enumerate(outs):
            out[side] = pre[offset(x, y + s)].astype(out.dtype)


def forward(at, half, blocks, weights):
    units, width = weights[0].shape
    part = jax.ShapeDtypeStruct((4, PART, units), BF16)
    return pl.pallas_call(
        functools.partial(forward_kernel, half),
        out_shape=(
            jax.ShapeDtypeStruct((NX * PART, width), BF16),
            jax.ShapeDtypeStruct((4, PART, units), F32),
            part,
            part,
            part,
        ),
        in_specs=[SMEM] + [VMEM] * 8,
        out_specs=(VMEM,) * 5,
        scratch_shapes=[pltpu.VMEM((NX, PART, units), F32)],
        compiler_params=PARAMS,
        cost_estimate=cost(0.1),
        name="forward%d" % half,
    )(at, *blocks, *weights)


def gradient_kernel(half, at_ref, own, from1, from2, from3, cot, cot_sibling, out, grad):
    x, c, zl = at_ref[0], at_ref[2], at_ref[3]
    for k, cotangent in enumerate((cot, cot_sibling)):
        for z in range(ZH):
            x_from = lax.rem(x - (z % 2) * NC - c + NX, NX)
            zl_from = lax.rem(zl + z // 2, ZL)
            grad[z * OWNED : (z + 1) * OWNED, :] = cotangent[x_from, zl_from, pl.ds(half * OWNED, OWNED), :]

        def total(side):
            near = own[side] + from1[side].astype(F32)
            return near + (from2[side].astype(F32) + from3[side].astype(F32))

        gate_pre, up_pre = total(2 * k), total(2 * k + 1)
        gate_sig = jax.nn.sigmoid(gate_pre)
        scaled = grad[...].astype(F32) * gate_sig
        out[2 * k] = (scaled * up_pre * (1.0 + gate_pre * (1.0 - gate_sig))).astype(BF16)
        out[2 * k + 1] = (scaled * gate_pre).astype(BF16)


def gradient(at, half, own, received, cot, cot_sibling):
    return pl.pallas_call(
        functools.partial(gradient_kernel, half),
        out_shape=jax.ShapeDtypeStruct(own.shape, BF16),
        in_specs=[SMEM] + [VMEM] * 6,
        out_specs=VMEM,
        scratch_shapes=[pltpu.VMEM(own.shape[1:], BF16)],
        compiler_params=PARAMS,
        cost_estimate=cost(0.1 + 6 * half),
        name="gradient%d" % half,
    )(at, own, *received, cot, cot_sibling)


def backward_kernel(tile, at_ref, own, from1, from2, from3, *refs):
    weights, fulls, outs = refs[:4], refs[4:6], refs[6:]
    x, y = at_ref[0], at_ref[1]
    for side in range(4):
        for s, ref in enumerate((own, from1, from2, from3)):
            fulls[side // 2][side % 2, offset(x, y - s)] = ref[side]
    rows = [fulls[side // 2][side % 2].reshape(NX * PART, own.shape[2]) for side in range(4)]
    for col in range(0, outs[0].shape[1], tile):
        total = None
        for side, weight in enumerate(weights):
            term = jnp.dot(rows[side], weight[:, col : col + tile], preferred_element_type=F32)
            total = term if total is None else total + term
        for o, out in enumerate(outs):
            out[:, col : col + tile] = total[o * PART : (o + 1) * PART].astype(out.dtype)


def backward(at, half, pieces, weights):
    units, width = weights[0].shape
    part = jax.ShapeDtypeStruct((PART, width), BF16)
    full = jax.ShapeDtypeStruct((2, NX, PART, units), BF16)
    return pl.pallas_call(
        functools.partial(backward_kernel, min(512, width)),
        out_shape=(
            full,
            full,
            jax.ShapeDtypeStruct((PART, width), F32),
            part,
            part,
            part,
        ),
        in_specs=[SMEM] + [VMEM] * 8,
        out_specs=(VMEM,) * 6,
        compiler_params=PARAMS,
        cost_estimate=cost(5),
        name="backward%d" % half,
    )(at, *pieces, *weights)


def weights_kernel(side, tile, *refs):
    n = len(refs) // 2
    tokens, fulls, out = refs[:n], refs[n : 2 * n], refs[-1]
    rows = jnp.concatenate([f[side].reshape(NX * PART, out.shape[0]) for f in fulls], axis=0)
    for col in range(0, out.shape[1], tile):
        total = lax.dot_general(
            rows,
            jnp.concatenate([r[:, col : col + tile] for r in tokens], axis=0),
            (((0,), (0,)), ((), ())),
            preferred_element_type=F32,
        )
        out[:, col : col + tile] = total.astype(BF16)


def weight_grad(tokens, fulls, side):
    width = tokens[0].shape[1]
    return pl.pallas_call(
        functools.partial(weights_kernel, side, min(512, width)),
        out_shape=jax.ShapeDtypeStruct((fulls[0].shape[3], width), BF16),
        in_specs=[VMEM] * (2 * len(tokens)),
        out_specs=VMEM,
        compiler_params=PARAMS,
        cost_estimate=cost(5),
        name="weight_grad%d" % side,
    )(*tokens, *fulls)


def halves_kernel(a, b, a_out, b_out):
    a_out[...] = a[: a_out.shape[0]]
    b_out[...] = b[b_out.shape[0] :]


def halves(a, b):
    rows, width = a.shape
    out = jax.ShapeDtypeStruct((rows // 2, width), a.dtype)
    return pl.pallas_call(
        halves_kernel,
        out_shape=(out, out),
        in_specs=[VMEM] * 2,
        out_specs=(VMEM, VMEM),
        compiler_params=PARAMS,
        cost_estimate=cost(0.1),
        name="halves",
    )(a, b)


def local(acts, gate_weight, up_weight, hidden_grad):
    rows, width = acts.shape
    units = gate_weight.shape[0]
    x, y, c, zl = lax.axis_index("x"), lax.axis_index("y"), lax.axis_index("c"), lax.axis_index("zl")
    at = jnp.stack([x, y, c, zl]).astype(jnp.int32)

    weights = [gate_weight, up_weight, core_swap(gate_weight), core_swap(up_weight)]

    cot = hidden_grad.reshape(ZL, NX, OWNED, ZL, NX, units)
    cot = lax.dynamic_index_in_dim(cot, y, 1, keepdims=False).reshape(ZL * OWNED, ZL, NX, units)
    cot = rolled(rolled(cot.transpose(1, 2, 0, 3), zl, 0), x, 1)

    mine = exchange(jnp.broadcast_to(acts[None], (ZL * ZH, rows, width)), ("zl", "zh")).reshape(BLOCK, width)
    mine, cot, *weights = lax.optimization_barrier((mine, cot, *weights))
    right = x_shift(mine, -1)
    left = x_shift(mine, 1)

    passed = shift(cot[1], "zl", 1, ZL)
    cot = [jnp.stack([cot[0, s], passed[s]]) for s in range(NX)]
    cot = jnp.stack([cot[0]] + [x_shift(cot[s], s) for s in range(1, NX)])

    right_half, left_half = halves(right, left)
    far = lax.optimization_barrier((x_shift(right_half, -1), x_shift(left_half, 1)))
    chunks = [[mine, right, f, left] for f in far]

    cot_sibling = core_swap(cot)
    tokens0, own0, *sent0 = forward(after(at, cot_sibling), 0, chunks[0], weights)
    got0 = [y_shift(t, s) for s, t in enumerate(sent0, 1)]
    tokens1, own1, *sent1 = forward(after(at, own0), 1, chunks[1], weights)
    got0, sent1 = lax.optimization_barrier((got0, sent1))
    got1 = [y_shift(t, s) for s, t in enumerate(sent1, 1)]
    grad0 = gradient(at, 0, own0, got0, cot, cot_sibling)
    pieces0 = [grad0] + [y_shift(grad0, s) for s in (1, 2, 3)]
    grad1 = gradient(after(at, grad0), 1, own1, got1, cot, cot_sibling)
    pieces1 = [grad1] + [y_shift(grad1, s) for s in (1, 2, 3)]

    full0, passed0, kept0, *parts0 = backward(after(at, grad1), 0, pieces0, weights)
    sums0 = [x_shift(part, o) for o, part in enumerate(parts0, 1)]
    full1, passed1, kept1, *parts1 = backward(after(at, kept0), 1, pieces1, weights)
    parts1, sums0 = lax.optimization_barrier((parts1, sums0))
    sums1 = [x_shift(part, o) for o, part in enumerate(parts1, 1)]

    totals = []
    for kept, sums in ((kept0, sums0), (kept1, sums1)):
        for part in sums:
            kept = kept + part.astype(F32)
        totals.append(kept.astype(BF16))
    total = jnp.concatenate(totals, axis=0)
    got = exchange(total.reshape(ZL * ZH, rows, width), ("zl", "zh"))
    tokens0, tokens1, kept1 = lax.optimization_barrier((tokens0, tokens1, kept1))
    tokens = [tokens0, tokens1, core_swap(tokens0), core_swap(tokens1)]
    fulls = [full0, full1, core_swap(passed0), core_swap(passed1)]
    gate_weight_grad, up_weight_grad = [weight_grad(tokens, fulls, side) for side in (0, 1)]
    got, gate_weight_grad, up_weight_grad = lax.optimization_barrier((got, gate_weight_grad, up_weight_grad))
    input_grad = got.astype(F32).sum(axis=0).astype(BF16)
    return input_grad, gate_weight_grad, up_weight_grad


def solution(mesh):
    fine = Mesh(np.asarray(mesh.devices).reshape(ZH, NC, NY, ZL, NX), ("zh", "c", "y", "zl", "x"))
    rows = ("zh", "c", "zl", "x")
    in_specs = (P(rows, "y"), P(rows, "y"), P(rows, "y"), P(("zl", "x"), ("zh", "c")))
    out_specs = (P(rows, "y"), P(rows, "y"), P(rows, "y"))
    return jax.shard_map(local, mesh=fine, in_specs=in_specs, out_specs=out_specs, check_vma=False)
```

```python
import functools

import jax
import jax.numpy as jnp
import numpy as np
from jax import lax
from jax.experimental import pallas as pl
from jax.experimental.pallas import tpu as pltpu
from jax.sharding import Mesh, PartitionSpec as P

F32 = jnp.float32
BF16 = jnp.bfloat16
NX, NY, ZH, ZL, NC = 4, 4, 4, 2, 2
OWNED = 16
BLOCK = ZL * ZH * OWNED
PART = ZH * OWNED


def cost(microseconds):
    return pl.CostEstimate(flops=int(1.1e9 * microseconds), bytes_accessed=1, transcendentals=0)


VMEM = pl.BlockSpec(memory_space=pltpu.VMEM)
SMEM = pl.BlockSpec(memory_space=pltpu.SMEM)
PARAMS = pltpu.CompilerParams(vmem_limit_bytes=16 * 2**20)


def shift(value, axis, by, size):
    return lax.ppermute(value, axis, [(i, (i + by) % size) for i in range(size)])


def x_shift(value, by):
    return shift(value, "x", by, NX)


def y_shift(value, by):
    return shift(value, "y", by, NY)


def core_swap(value):
    return shift(value, "c", 1, NC)


def exchange(value, axes):
    return lax.all_to_all(value, axes, split_axis=0, concat_axis=0, tiled=True)


def rolled(value, by, axis):
    size = value.shape[axis]
    twice = jnp.concatenate([value, value], axis=axis)
    return lax.dynamic_slice_in_dim(twice, by, size, axis)


def after(value, *others):
    return lax.optimization_barrier((value,) + others)[0]


def offset(x, owner):
    return lax.rem(owner - x + 2 * NX, NX)


def part_of(ref, half):
    return ref[...] if ref.shape[0] == PART else ref[half * PART : (half + 1) * PART]


def forward_kernel(half, at_ref, *refs):
    blocks, weights, tokens, outs, pre = refs[:NX], refs[NX : NX + 4], refs[NX + 4], refs[NX + 5 : -1], refs[-1]
    x, y = at_ref[0], at_ref[1]
    for o, block in enumerate(blocks):
        tokens[o * PART : (o + 1) * PART] = part_of(block, half)
    for side, weight in enumerate(weights):
        value = lax.dot_general(tokens[...], weight[...], (((1,), (1,)), ((), ())), preferred_element_type=F32)
        for o in range(NX):
            pre[o] = value[o * PART : (o + 1) * PART]
        for s, out in enumerate(outs):
            out[side] = pre[offset(x, y + s)].astype(out.dtype)


def forward(at, half, blocks, weights):
    units, width = weights[0].shape
    part = jax.ShapeDtypeStruct((4, PART, units), BF16)
    return pl.pallas_call(
        functools.partial(forward_kernel, half),
        out_shape=(
            jax.ShapeDtypeStruct((NX * PART, width), BF16),
            jax.ShapeDtypeStruct((4, PART, units), F32),
            part,
            part,
            part,
        ),
        in_specs=[SMEM] + [VMEM] * 8,
        out_specs=(VMEM,) * 5,
        scratch_shapes=[pltpu.VMEM((NX, PART, units), F32)],
        compiler_params=PARAMS,
        cost_estimate=cost(0.1),
        name="forward%d" % half,
    )(at, *blocks, *weights)


def gradient_kernel(half, at_ref, own, from1, from2, from3, cot, cot_sibling, out, grad):
    x, c, zl = at_ref[0], at_ref[2], at_ref[3]
    for k, cotangent in enumerate((cot, cot_sibling)):
        for z in range(ZH):
            x_from = lax.rem(x - (z % 2) * NC - c + NX, NX)
            zl_from = lax.rem(zl + z // 2, ZL)
            grad[z * OWNED : (z + 1) * OWNED, :] = cotangent[x_from, zl_from, pl.ds(half * OWNED, OWNED), :]

        def total(side):
            near = own[side] + from1[side].astype(F32)
            return near + (from2[side].astype(F32) + from3[side].astype(F32))

        gate_pre, up_pre = total(2 * k), total(2 * k + 1)
        gate_sig = jax.nn.sigmoid(gate_pre)
        scaled = grad[...].astype(F32) * gate_sig
        out[2 * k] = (scaled * up_pre * (1.0 + gate_pre * (1.0 - gate_sig))).astype(BF16)
        out[2 * k + 1] = (scaled * gate_pre).astype(BF16)


def gradient(at, half, own, received, cot, cot_sibling):
    return pl.pallas_call(
        functools.partial(gradient_kernel, half),
        out_shape=jax.ShapeDtypeStruct(own.shape, BF16),
        in_specs=[SMEM] + [VMEM] * 6,
        out_specs=VMEM,
        scratch_shapes=[pltpu.VMEM(own.shape[1:], BF16)],
        compiler_params=PARAMS,
        cost_estimate=cost(0.1 + 6 * half),
        name="gradient%d" % half,
    )(at, own, *received, cot, cot_sibling)


def backward_kernel(tile, at_ref, own, from1, from2, from3, *refs):
    weights, fulls, outs = refs[:4], refs[4:6], refs[6:]
    x, y = at_ref[0], at_ref[1]
    for side in range(4):
        for s, ref in enumerate((own, from1, from2, from3)):
            fulls[side // 2][side % 2, offset(x, y - s)] = ref[side]
    rows = [fulls[side // 2][side % 2].reshape(NX * PART, own.shape[2]) for side in range(4)]
    for col in range(0, outs[0].shape[1], tile):
        total = None
        for side, weight in enumerate(weights):
            term = jnp.dot(rows[side], weight[:, col : col + tile], preferred_element_type=F32)
            total = term if total is None else total + term
        for o, out in enumerate(outs):
            out[:, col : col + tile] = total[o * PART : (o + 1) * PART].astype(out.dtype)


def backward(at, half, pieces, weights):
    units, width = weights[0].shape
    part = jax.ShapeDtypeStruct((PART, width), BF16)
    full = jax.ShapeDtypeStruct((2, NX, PART, units), BF16)
    return pl.pallas_call(
        functools.partial(backward_kernel, min(512, width)),
        out_shape=(
            full,
            full,
            jax.ShapeDtypeStruct((PART, width), F32),
            part,
            part,
            part,
        ),
        in_specs=[SMEM] + [VMEM] * 8,
        out_specs=(VMEM,) * 6,
        compiler_params=PARAMS,
        cost_estimate=cost(5),
        name="backward%d" % half,
    )(at, *pieces, *weights)


def weights_kernel(tile, *refs):
    tokens, fulls, outs = refs[:4], refs[4:8], refs[8:]
    for side, out in enumerate(outs):
        rows = jnp.concatenate([f[side].reshape(NX * PART, out.shape[0]) for f in fulls], axis=0)
        for col in range(0, out.shape[1], tile):
            total = lax.dot_general(
                rows,
                jnp.concatenate([r[:, col : col + tile] for r in tokens], axis=0),
                (((0,), (0,)), ((), ())),
                preferred_element_type=F32,
            )
            out[:, col : col + tile] = total.astype(BF16)


def weight_grads(tokens, fulls):
    width = tokens[0].shape[1]
    out = jax.ShapeDtypeStruct((fulls[0].shape[3], width), BF16)
    return pl.pallas_call(
        functools.partial(weights_kernel, min(512, width)),
        out_shape=(out, out),
        in_specs=[VMEM] * 8,
        out_specs=(VMEM, VMEM),
        compiler_params=PARAMS,
        cost_estimate=cost(10),
        name="weight_grads",
    )(*tokens, *fulls)


def halves_kernel(a, b, a_out, b_out):
    a_out[...] = a[: a_out.shape[0]]
    b_out[...] = b[b_out.shape[0] :]


def halves(a, b):
    rows, width = a.shape
    out = jax.ShapeDtypeStruct((rows // 2, width), a.dtype)
    return pl.pallas_call(
        halves_kernel,
        out_shape=(out, out),
        in_specs=[VMEM] * 2,
        out_specs=(VMEM, VMEM),
        compiler_params=PARAMS,
        cost_estimate=cost(0.1),
        name="halves",
    )(a, b)


def add_up_kernel(got, out):
    total = got[0].astype(F32)
    for z in range(1, got.shape[0]):
        total = total + got[z].astype(F32)
    out[...] = total.astype(BF16)


def add_up(got):
    return pl.pallas_call(
        add_up_kernel,
        out_shape=jax.ShapeDtypeStruct(got.shape[1:], BF16),
        in_specs=[VMEM],
        out_specs=VMEM,
        compiler_params=PARAMS,
        cost_estimate=cost(0.1),
        name="add_up",
    )(got)


def local(acts, gate_weight, up_weight, hidden_grad):
    rows, width = acts.shape
    units = gate_weight.shape[0]
    x, y, c, zl = lax.axis_index("x"), lax.axis_index("y"), lax.axis_index("c"), lax.axis_index("zl")
    at = jnp.stack([x, y, c, zl]).astype(jnp.int32)

    weights = [gate_weight, up_weight, core_swap(gate_weight), core_swap(up_weight)]

    cot = hidden_grad.reshape(ZL, NX, OWNED, ZL, NX, units)
    cot = lax.dynamic_index_in_dim(cot, y, 1, keepdims=False).reshape(ZL * OWNED, ZL, NX, units)
    cot = rolled(rolled(cot.transpose(1, 2, 0, 3), zl, 0), x, 1)

    mine = exchange(jnp.broadcast_to(acts[None], (ZL * ZH, rows, width)), ("zl", "zh")).reshape(BLOCK, width)
    mine, cot, *weights = lax.optimization_barrier((mine, cot, *weights))
    right = x_shift(mine, -1)
    left = x_shift(mine, 1)

    passed = shift(cot[1], "zl", 1, ZL)
    cot = [jnp.stack([cot[0, s], passed[s]]) for s in range(NX)]
    cot = jnp.stack([cot[0]] + [x_shift(cot[s], s) for s in range(1, NX)])

    right_half, left_half = halves(right, left)
    far = lax.optimization_barrier((x_shift(right_half, -1), x_shift(left_half, 1)))
    chunks = [[mine, right, f, left] for f in far]

    cot_sibling = core_swap(cot)
    tokens0, own0, *sent0 = forward(after(at, cot_sibling), 0, chunks[0], weights)
    got0 = [y_shift(t, s) for s, t in enumerate(sent0, 1)]
    tokens1, own1, *sent1 = forward(after(at, own0), 1, chunks[1], weights)
    got0, sent1 = lax.optimization_barrier((got0, sent1))
    got1 = [y_shift(t, s) for s, t in enumerate(sent1, 1)]
    grad0 = gradient(at, 0, own0, got0, cot, cot_sibling)
    pieces0 = [grad0] + [y_shift(grad0, s) for s in (1, 2, 3)]
    grad1 = gradient(after(at, grad0), 1, own1, got1, cot, cot_sibling)
    pieces1 = [grad1] + [y_shift(grad1, s) for s in (1, 2, 3)]

    full0, passed0, kept0, *parts0 = backward(after(at, grad1), 0, pieces0, weights)
    sums0 = [x_shift(part, o) for o, part in enumerate(parts0, 1)]
    full1, passed1, kept1, *parts1 = backward(after(at, kept0), 1, pieces1, weights)
    parts1, sums0[0], sums0[2] = lax.optimization_barrier((parts1, sums0[0], sums0[2]))
    sums1 = [x_shift(part, o) for o, part in enumerate(parts1, 1)]

    totals = []
    for kept, sums in ((kept0, sums0), (kept1, sums1)):
        for part in sums:
            kept = kept + part.astype(F32)
        totals.append(kept.astype(BF16))
    total = jnp.concatenate(totals, axis=0)
    got = exchange(total.reshape(ZL * ZH, rows, width), ("zl", "zh"))
    tokens0, tokens1, kept1 = lax.optimization_barrier((tokens0, tokens1, kept1))
    tokens = [tokens0, tokens1, core_swap(tokens0), core_swap(tokens1)]
    fulls = [full0, full1, core_swap(passed0), core_swap(passed1)]
    gate_weight_grad, up_weight_grad = weight_grads(tokens, fulls)
    got, gate_weight_grad, up_weight_grad = lax.optimization_barrier((got, gate_weight_grad, up_weight_grad))
    input_grad = add_up(got)
    return input_grad, gate_weight_grad, up_weight_grad


def solution(mesh):
    fine = Mesh(np.asarray(mesh.devices).reshape(ZH, NC, NY, ZL, NX), ("zh", "c", "y", "zl", "x"))
    rows = ("zh", "c", "zl", "x")
    in_specs = (P(rows, "y"), P(rows, "y"), P(rows, "y"), P(("zl", "x"), ("zh", "c")))
    out_specs = (P(rows, "y"), P(rows, "y"), P(rows, "y"))
    return jax.shard_map(local, mesh=fine, in_specs=in_specs, out_specs=out_specs, check_vma=False)
```

```python
import functools

import jax
import jax.numpy as jnp
import numpy as np
from jax import lax
from jax.experimental import pallas as pl
from jax.experimental.pallas import tpu as pltpu
from jax.sharding import Mesh, PartitionSpec as P

F32 = jnp.float32
BF16 = jnp.bfloat16
NX, NY, ZH, ZL, NC = 4, 4, 4, 2, 2
OWNED = 16
BLOCK = ZL * ZH * OWNED
PART = ZH * OWNED


def cost(microseconds):
    return pl.CostEstimate(flops=int(1.1e9 * microseconds), bytes_accessed=1, transcendentals=0)


VMEM = pl.BlockSpec(memory_space=pltpu.VMEM)
SMEM = pl.BlockSpec(memory_space=pltpu.SMEM)
PARAMS = pltpu.CompilerParams(vmem_limit_bytes=16 * 2**20)


def shift(value, axis, by, size):
    return lax.ppermute(value, axis, [(i, (i + by) % size) for i in range(size)])


def x_shift(value, by):
    return shift(value, "x", by, NX)


def y_shift(value, by):
    return shift(value, "y", by, NY)


def core_swap(value):
    return shift(value, "c", 1, NC)


def exchange(value, axes):
    return lax.all_to_all(value, axes, split_axis=0, concat_axis=0, tiled=True)


def rolled(value, by, axis):
    size = value.shape[axis]
    twice = jnp.concatenate([value, value], axis=axis)
    return lax.dynamic_slice_in_dim(twice, by, size, axis)


def after(value, *others):
    return lax.optimization_barrier((value,) + others)[0]


def offset(x, owner):
    return lax.rem(owner - x + 2 * NX, NX)


def part_of(ref, half):
    return ref[...] if ref.shape[0] == PART else ref[half * PART : (half + 1) * PART]


def forward_kernel(half, at_ref, *refs):
    blocks, weights, tokens, outs, pre = refs[:NX], refs[NX : NX + 4], refs[NX + 4], refs[NX + 5 : -1], refs[-1]
    x, y = at_ref[0], at_ref[1]
    for o, block in enumerate(blocks):
        tokens[o * PART : (o + 1) * PART] = part_of(block, half)
    for side, weight in enumerate(weights):
        value = lax.dot_general(tokens[...], weight[...], (((1,), (1,)), ((), ())), preferred_element_type=F32)
        for o in range(NX):
            pre[o] = value[o * PART : (o + 1) * PART]
        for s, out in enumerate(outs):
            out[side] = pre[offset(x, y + s)].astype(out.dtype)


def forward(at, half, blocks, weights):
    units, width = weights[0].shape
    part = jax.ShapeDtypeStruct((4, PART, units), BF16)
    return pl.pallas_call(
        functools.partial(forward_kernel, half),
        out_shape=(
            jax.ShapeDtypeStruct((NX * PART, width), BF16),
            jax.ShapeDtypeStruct((4, PART, units), F32),
            part,
            part,
            part,
        ),
        in_specs=[SMEM] + [VMEM] * 8,
        out_specs=(VMEM,) * 5,
        scratch_shapes=[pltpu.VMEM((NX, PART, units), F32)],
        compiler_params=PARAMS,
        cost_estimate=cost(0.1),
        name="forward%d" % half,
    )(at, *blocks, *weights)


def gradient_kernel(half, at_ref, own, from1, from2, from3, cot, cot_sibling, out, grad):
    x, c, zl = at_ref[0], at_ref[2], at_ref[3]
    for k, cotangent in enumerate((cot, cot_sibling)):
        for z in range(ZH):
            x_from = lax.rem(x - (z % 2) * NC - c + NX, NX)
            zl_from = lax.rem(zl + z // 2, ZL)
            grad[z * OWNED : (z + 1) * OWNED, :] = cotangent[x_from, zl_from, pl.ds(half * OWNED, OWNED), :]

        def total(side):
            near = own[side] + from1[side].astype(F32)
            return near + (from2[side].astype(F32) + from3[side].astype(F32))

        gate_pre, up_pre = total(2 * k), total(2 * k + 1)
        gate_sig = jax.nn.sigmoid(gate_pre)
        scaled = grad[...].astype(F32) * gate_sig
        out[2 * k] = (scaled * up_pre * (1.0 + gate_pre * (1.0 - gate_sig))).astype(BF16)
        out[2 * k + 1] = (scaled * gate_pre).astype(BF16)


def gradient(at, half, own, received, cot, cot_sibling):
    return pl.pallas_call(
        functools.partial(gradient_kernel, half),
        out_shape=jax.ShapeDtypeStruct(own.shape, BF16),
        in_specs=[SMEM] + [VMEM] * 6,
        out_specs=VMEM,
        scratch_shapes=[pltpu.VMEM(own.shape[1:], BF16)],
        compiler_params=PARAMS,
        cost_estimate=cost(0.1 + 6 * half),
        name="gradient%d" % half,
    )(at, own, *received, cot, cot_sibling)


def backward_kernel(tile, at_ref, own, from1, from2, from3, *refs):
    weights, fulls, outs = refs[:4], refs[4:6], refs[6:]
    x, y = at_ref[0], at_ref[1]
    for side in range(4):
        for s, ref in enumerate((own, from1, from2, from3)):
            fulls[side // 2][side % 2, offset(x, y - s)] = ref[side]
    rows = [fulls[side // 2][side % 2].reshape(NX * PART, own.shape[2]) for side in range(4)]
    for col in range(0, outs[0].shape[1], tile):
        total = None
        for side, weight in enumerate(weights):
            term = jnp.dot(rows[side], weight[:, col : col + tile], preferred_element_type=F32)
            total = term if total is None else total + term
        for o, out in enumerate(outs):
            out[:, col : col + tile] = total[o * PART : (o + 1) * PART].astype(out.dtype)


def backward(at, half, pieces, weights):
    units, width = weights[0].shape
    part = jax.ShapeDtypeStruct((PART, width), BF16)
    full = jax.ShapeDtypeStruct((2, NX, PART, units), BF16)
    return pl.pallas_call(
        functools.partial(backward_kernel, min(512, width)),
        out_shape=(
            full,
            full,
            jax.ShapeDtypeStruct((PART, width), F32),
            part,
            part,
            part,
        ),
        in_specs=[SMEM] + [VMEM] * 8,
        out_specs=(VMEM,) * 6,
        compiler_params=PARAMS,
        cost_estimate=cost(5),
        name="backward%d" % half,
    )(at, *pieces, *weights)


def weights_kernel(tile, *refs):
    tokens, fulls, outs = refs[:4], refs[4:8], refs[8:]
    for side, out in enumerate(outs):
        rows = jnp.concatenate([f[side].reshape(NX * PART, out.shape[0]) for f in fulls], axis=0)
        for col in range(0, out.shape[1], tile):
            total = lax.dot_general(
                rows,
                jnp.concatenate([r[:, col : col + tile] for r in tokens], axis=0),
                (((0,), (0,)), ((), ())),
                preferred_element_type=F32,
            )
            out[:, col : col + tile] = total.astype(BF16)


def weight_grads(tokens, fulls):
    width = tokens[0].shape[1]
    out = jax.ShapeDtypeStruct((fulls[0].shape[3], width), BF16)
    return pl.pallas_call(
        functools.partial(weights_kernel, min(512, width)),
        out_shape=(out, out),
        in_specs=[VMEM] * 8,
        out_specs=(VMEM, VMEM),
        compiler_params=PARAMS,
        cost_estimate=cost(10),
        name="weight_grads",
    )(*tokens, *fulls)


def halves_kernel(a, b, a_out, b_out):
    a_out[...] = a[: a_out.shape[0]]
    b_out[...] = b[b_out.shape[0] :]


def halves(a, b):
    rows, width = a.shape
    out = jax.ShapeDtypeStruct((rows // 2, width), a.dtype)
    return pl.pallas_call(
        halves_kernel,
        out_shape=(out, out),
        in_specs=[VMEM] * 2,
        out_specs=(VMEM, VMEM),
        compiler_params=PARAMS,
        cost_estimate=cost(0.1),
        name="halves",
    )(a, b)


def add_up_kernel(got, out):
    total = got[0].astype(F32)
    for z in range(1, got.shape[0]):
        total = total + got[z].astype(F32)
    out[...] = total.astype(BF16)


def add_up(got):
    return pl.pallas_call(
        add_up_kernel,
        out_shape=jax.ShapeDtypeStruct(got.shape[1:], BF16),
        in_specs=[VMEM],
        out_specs=VMEM,
        compiler_params=PARAMS,
        cost_estimate=cost(0.1),
        name="add_up",
    )(got)


def local(acts, gate_weight, up_weight, hidden_grad):
    rows, width = acts.shape
    units = gate_weight.shape[0]
    x, y, c, zl = lax.axis_index("x"), lax.axis_index("y"), lax.axis_index("c"), lax.axis_index("zl")
    at = jnp.stack([x, y, c, zl]).astype(jnp.int32)

    weights = [gate_weight, up_weight, core_swap(gate_weight), core_swap(up_weight)]

    cot = hidden_grad.reshape(ZL, NX, OWNED, ZL, NX, units)
    cot = lax.dynamic_index_in_dim(cot, y, 1, keepdims=False).reshape(ZL * OWNED, ZL, NX, units)
    cot = rolled(rolled(cot.transpose(1, 2, 0, 3), zl, 0), x, 1)

    mine = exchange(jnp.broadcast_to(acts[None], (ZL * ZH, rows, width)), ("zl", "zh")).reshape(BLOCK, width)
    mine, cot, *weights = lax.optimization_barrier((mine, cot, *weights))
    right = x_shift(mine, -1)
    left = x_shift(mine, 1)

    passed = shift(cot[1], "zl", 1, ZL)
    cot = [jnp.stack([cot[0, s], passed[s]]) for s in range(NX)]
    cot = jnp.stack([cot[0]] + [x_shift(cot[s], s) for s in range(1, NX)])

    right_half, left_half = halves(right, left)
    far = lax.optimization_barrier((x_shift(right_half, -1), x_shift(left_half, 1)))
    chunks = [[mine, right, f, left] for f in far]

    cot_sibling = core_swap(cot)
    tokens0, own0, *sent0 = forward(after(at, cot_sibling), 0, chunks[0], weights)
    got0 = [y_shift(t, s) for s, t in enumerate(sent0, 1)]
    tokens1, own1, *sent1 = forward(after(at, own0), 1, chunks[1], weights)
    got0[0], got0[2], sent1 = lax.optimization_barrier((got0[0], got0[2], sent1))
    got1 = [y_shift(t, s) for s, t in enumerate(sent1, 1)]
    grad0 = gradient(at, 0, own0, got0, cot, cot_sibling)
    pieces0 = [grad0] + [y_shift(grad0, s) for s in (1, 2, 3)]
    grad1 = gradient(after(at, grad0), 1, own1, got1, cot, cot_sibling)
    pieces1 = [grad1] + [y_shift(grad1, s) for s in (1, 2, 3)]

    full0, passed0, kept0, *parts0 = backward(after(at, grad1), 0, pieces0, weights)
    sums0 = [x_shift(part, o) for o, part in enumerate(parts0, 1)]
    full1, passed1, kept1, *parts1 = backward(after(at, kept0), 1, pieces1, weights)
    parts1, sums0[0], sums0[2] = lax.optimization_barrier((parts1, sums0[0], sums0[2]))
    sums1 = [x_shift(part, o) for o, part in enumerate(parts1, 1)]

    totals = []
    for kept, sums in ((kept0, sums0), (kept1, sums1)):
        for part in sums:
            kept = kept + part.astype(F32)
        totals.append(kept.astype(BF16))
    total = jnp.concatenate(totals, axis=0)
    got = exchange(total.reshape(ZL * ZH, rows, width), ("zl", "zh"))
    tokens0, tokens1, kept1 = lax.optimization_barrier((tokens0, tokens1, kept1))
    tokens = [tokens0, tokens1, core_swap(tokens0), core_swap(tokens1)]
    fulls = [full0, full1, core_swap(passed0), core_swap(passed1)]
    gate_weight_grad, up_weight_grad = weight_grads(tokens, fulls)
    got, gate_weight_grad, up_weight_grad = lax.optimization_barrier((got, gate_weight_grad, up_weight_grad))
    input_grad = add_up(got)
    return input_grad, gate_weight_grad, up_weight_grad


def solution(mesh):
    fine = Mesh(np.asarray(mesh.devices).reshape(ZH, NC, NY, ZL, NX), ("zh", "c", "y", "zl", "x"))
    rows = ("zh", "c", "zl", "x")
    in_specs = (P(rows, "y"), P(rows, "y"), P(rows, "y"), P(("zl", "x"), ("zh", "c")))
    out_specs = (P(rows, "y"), P(rows, "y"), P(rows, "y"))
    return jax.shard_map(local, mesh=fine, in_specs=in_specs, out_specs=out_specs, check_vma=False)
```

```python
import functools

import jax
import jax.numpy as jnp
import numpy as np
from jax import lax
from jax.experimental import pallas as pl
from jax.experimental.pallas import tpu as pltpu
from jax.sharding import Mesh, PartitionSpec as P

F32 = jnp.float32
BF16 = jnp.bfloat16
NX, NY, ZH, ZL, NC = 4, 4, 4, 2, 2
OWNED = 16
BLOCK = ZL * ZH * OWNED
PART = ZH * OWNED


def cost(microseconds):
    return pl.CostEstimate(flops=int(1.1e9 * microseconds), bytes_accessed=1, transcendentals=0)


VMEM = pl.BlockSpec(memory_space=pltpu.VMEM)
SMEM = pl.BlockSpec(memory_space=pltpu.SMEM)
PARAMS = pltpu.CompilerParams(vmem_limit_bytes=16 * 2**20)


def shift(value, axis, by, size):
    return lax.ppermute(value, axis, [(i, (i + by) % size) for i in range(size)])


def x_shift(value, by):
    return shift(value, "x", by, NX)


def y_shift(value, by):
    return shift(value, "y", by, NY)


def core_swap(value):
    return shift(value, "c", 1, NC)


def exchange(value, axes):
    return lax.all_to_all(value, axes, split_axis=0, concat_axis=0, tiled=True)


def rolled(value, by, axis):
    size = value.shape[axis]
    twice = jnp.concatenate([value, value], axis=axis)
    return lax.dynamic_slice_in_dim(twice, by, size, axis)


def after(value, *others):
    return lax.optimization_barrier((value,) + others)[0]


def offset(x, owner):
    return lax.rem(owner - x + 2 * NX, NX)


def part_of(ref, half):
    return ref[...] if ref.shape[0] == PART else ref[half * PART : (half + 1) * PART]


def forward_kernel(half, at_ref, *refs):
    blocks, weights, tokens, outs, pre = refs[:NX], refs[NX : NX + 4], refs[NX + 4], refs[NX + 5 : -1], refs[-1]
    x, y = at_ref[0], at_ref[1]
    for o, block in enumerate(blocks):
        tokens[o * PART : (o + 1) * PART] = part_of(block, half)
    for side, weight in enumerate(weights):
        value = lax.dot_general(tokens[...], weight[...], (((1,), (1,)), ((), ())), preferred_element_type=F32)
        for o in range(NX):
            pre[o] = value[o * PART : (o + 1) * PART]
        for s, out in enumerate(outs):
            out[side] = pre[offset(x, y + s)].astype(out.dtype)


def forward(at, half, blocks, weights):
    units, width = weights[0].shape
    part = jax.ShapeDtypeStruct((4, PART, units), BF16)
    return pl.pallas_call(
        functools.partial(forward_kernel, half),
        out_shape=(
            jax.ShapeDtypeStruct((NX * PART, width), BF16),
            jax.ShapeDtypeStruct((4, PART, units), F32),
            part,
            part,
            part,
        ),
        in_specs=[SMEM] + [VMEM] * 8,
        out_specs=(VMEM,) * 5,
        scratch_shapes=[pltpu.VMEM((NX, PART, units), F32)],
        compiler_params=PARAMS,
        cost_estimate=cost(0.1),
        name="forward%d" % half,
    )(at, *blocks, *weights)


def gradient_kernel(half, at_ref, own, from1, from2, from3, cot, cot_sibling, out, grad):
    x, c, zl = at_ref[0], at_ref[2], at_ref[3]
    for k, cotangent in enumerate((cot, cot_sibling)):
        for z in range(ZH):
            x_from = lax.rem(x - (z % 2) * NC - c + NX, NX)
            zl_from = lax.rem(zl + z // 2, ZL)
            grad[z * OWNED : (z + 1) * OWNED, :] = cotangent[x_from, zl_from, pl.ds(half * OWNED, OWNED), :]

        def total(side):
            near = own[side] + from1[side].astype(F32)
            return near + (from2[side].astype(F32) + from3[side].astype(F32))

        gate_pre, up_pre = total(2 * k), total(2 * k + 1)
        gate_sig = jax.nn.sigmoid(gate_pre)
        scaled = grad[...].astype(F32) * gate_sig
        out[2 * k] = (scaled * up_pre * (1.0 + gate_pre * (1.0 - gate_sig))).astype(BF16)
        out[2 * k + 1] = (scaled * gate_pre).astype(BF16)


def gradient(at, half, own, received, cot, cot_sibling):
    return pl.pallas_call(
        functools.partial(gradient_kernel, half),
        out_shape=jax.ShapeDtypeStruct(own.shape, BF16),
        in_specs=[SMEM] + [VMEM] * 6,
        out_specs=VMEM,
        scratch_shapes=[pltpu.VMEM(own.shape[1:], BF16)],
        compiler_params=PARAMS,
        cost_estimate=cost(0.1 + 6 * half),
        name="gradient%d" % half,
    )(at, own, *received, cot, cot_sibling)


def backward_kernel(tile, at_ref, own, from1, from2, from3, *refs):
    weights, fulls, outs = refs[:4], refs[4:6], refs[6:]
    x, y = at_ref[0], at_ref[1]
    for side in range(4):
        for s, ref in enumerate((own, from1, from2, from3)):
            fulls[side // 2][side % 2, offset(x, y - s)] = ref[side]
    rows = [fulls[side // 2][side % 2].reshape(NX * PART, own.shape[2]) for side in range(4)]
    for col in range(0, outs[0].shape[1], tile):
        total = None
        for side, weight in enumerate(weights):
            term = jnp.dot(rows[side], weight[:, col : col + tile], preferred_element_type=F32)
            total = term if total is None else total + term
        for o, out in enumerate(outs):
            out[:, col : col + tile] = total[o * PART : (o + 1) * PART].astype(out.dtype)


def backward(at, half, pieces, weights):
    units, width = weights[0].shape
    part = jax.ShapeDtypeStruct((PART, width), BF16)
    full = jax.ShapeDtypeStruct((2, NX, PART, units), BF16)
    return pl.pallas_call(
        functools.partial(backward_kernel, min(512, width)),
        out_shape=(
            full,
            full,
            jax.ShapeDtypeStruct((PART, width), F32),
            part,
            part,
            part,
        ),
        in_specs=[SMEM] + [VMEM] * 8,
        out_specs=(VMEM,) * 6,
        compiler_params=PARAMS,
        cost_estimate=cost(5),
        name="backward%d" % half,
    )(at, *pieces, *weights)


def weights_kernel(tile, *refs):
    tokens, fulls, outs = refs[:4], refs[4:8], refs[8:]
    for side, out in enumerate(outs):
        rows = jnp.concatenate([f[side].reshape(NX * PART, out.shape[0]) for f in fulls], axis=0)
        for col in range(0, out.shape[1], tile):
            total = lax.dot_general(
                rows,
                jnp.concatenate([r[:, col : col + tile] for r in tokens], axis=0),
                (((0,), (0,)), ((), ())),
                preferred_element_type=F32,
            )
            out[:, col : col + tile] = total.astype(BF16)


def weight_grads(tokens, fulls):
    width = tokens[0].shape[1]
    out = jax.ShapeDtypeStruct((fulls[0].shape[3], width), BF16)
    return pl.pallas_call(
        functools.partial(weights_kernel, min(512, width)),
        out_shape=(out, out),
        in_specs=[VMEM] * 8,
        out_specs=(VMEM, VMEM),
        compiler_params=PARAMS,
        cost_estimate=cost(10),
        name="weight_grads",
    )(*tokens, *fulls)


def halves_kernel(a, b, a_out, b_out):
    a_out[...] = a[: a_out.shape[0]]
    b_out[...] = b[b_out.shape[0] :]


def halves(a, b):
    rows, width = a.shape
    out = jax.ShapeDtypeStruct((rows // 2, width), a.dtype)
    return pl.pallas_call(
        halves_kernel,
        out_shape=(out, out),
        in_specs=[VMEM] * 2,
        out_specs=(VMEM, VMEM),
        compiler_params=PARAMS,
        cost_estimate=cost(0.1),
        name="halves",
    )(a, b)


def add_up_kernel(got, out):
    total = got[0].astype(F32)
    for z in range(1, got.shape[0]):
        total = total + got[z].astype(F32)
    out[...] = total.astype(BF16)


def add_up(got):
    return pl.pallas_call(
        add_up_kernel,
        out_shape=jax.ShapeDtypeStruct(got.shape[1:], BF16),
        in_specs=[VMEM],
        out_specs=VMEM,
        compiler_params=PARAMS,
        cost_estimate=cost(0.1),
        name="add_up",
    )(got)


def local(acts, gate_weight, up_weight, hidden_grad):
    rows, width = acts.shape
    units = gate_weight.shape[0]
    x, y, c, zl = lax.axis_index("x"), lax.axis_index("y"), lax.axis_index("c"), lax.axis_index("zl")
    at = jnp.stack([x, y, c, zl]).astype(jnp.int32)

    weights = [gate_weight, up_weight, core_swap(gate_weight), core_swap(up_weight)]

    cot = hidden_grad.reshape(ZL, NX, OWNED, ZL, NX, units)
    cot = lax.dynamic_index_in_dim(cot, y, 1, keepdims=False).reshape(ZL * OWNED, ZL, NX, units)
    cot = rolled(rolled(cot.transpose(1, 2, 0, 3), zl, 0), x, 1)

    mine = exchange(jnp.broadcast_to(acts[None], (ZL * ZH, rows, width)), ("zl", "zh")).reshape(BLOCK, width)
    mine, cot, *weights = lax.optimization_barrier((mine, cot, *weights))
    right = x_shift(mine, -1)
    left = x_shift(mine, 1)

    passed = shift(cot[1], "zl", 1, ZL)
    cot = [jnp.stack([cot[0, s], passed[s]]) for s in range(NX)]
    cot = jnp.stack([cot[0]] + [x_shift(cot[s], s) for s in range(1, NX)])

    right_half, left_half = halves(right, left)
    far = lax.optimization_barrier((x_shift(right_half, -1), x_shift(left_half, 1)))
    chunks = [[mine, right, f, left] for f in far]

    cot_sibling = core_swap(cot)
    tokens0, own0, *sent0 = forward(after(at, cot_sibling), 0, chunks[0], weights)
    got0 = [y_shift(t, s) for s, t in enumerate(sent0, 1)]
    tokens1, own1, *sent1 = forward(after(at, own0), 1, chunks[1], weights)
    got0[2], sent1 = lax.optimization_barrier((got0[2], sent1))
    got1 = [y_shift(t, s) for s, t in enumerate(sent1, 1)]
    grad0 = gradient(at, 0, own0, got0, cot, cot_sibling)
    pieces0 = [grad0] + [y_shift(grad0, s) for s in (1, 2, 3)]
    grad1 = gradient(after(at, grad0), 1, own1, got1, cot, cot_sibling)
    pieces1 = [grad1] + [y_shift(grad1, s) for s in (1, 2, 3)]

    full0, passed0, kept0, *parts0 = backward(after(at, grad1), 0, pieces0, weights)
    sums0 = [x_shift(part, o) for o, part in enumerate(parts0, 1)]
    full1, passed1, kept1, *parts1 = backward(after(at, kept0), 1, pieces1, weights)
    parts1, sums0[0], sums0[2] = lax.optimization_barrier((parts1, sums0[0], sums0[2]))
    sums1 = [x_shift(part, o) for o, part in enumerate(parts1, 1)]

    totals = []
    for kept, sums in ((kept0, sums0), (kept1, sums1)):
        for part in sums:
            kept = kept + part.astype(F32)
        totals.append(kept.astype(BF16))
    total = jnp.concatenate(totals, axis=0)
    got = exchange(total.reshape(ZL * ZH, rows, width), ("zl", "zh"))
    tokens0, tokens1, kept1 = lax.optimization_barrier((tokens0, tokens1, kept1))
    tokens = [tokens0, tokens1, core_swap(tokens0), core_swap(tokens1)]
    fulls = [full0, full1, core_swap(passed0), core_swap(passed1)]
    gate_weight_grad, up_weight_grad = weight_grads(tokens, fulls)
    got, gate_weight_grad, up_weight_grad = lax.optimization_barrier((got, gate_weight_grad, up_weight_grad))
    input_grad = add_up(got)
    return input_grad, gate_weight_grad, up_weight_grad


def solution(mesh):
    fine = Mesh(np.asarray(mesh.devices).reshape(ZH, NC, NY, ZL, NX), ("zh", "c", "y", "zl", "x"))
    rows = ("zh", "c", "zl", "x")
    in_specs = (P(rows, "y"), P(rows, "y"), P(rows, "y"), P(("zl", "x"), ("zh", "c")))
    out_specs = (P(rows, "y"), P(rows, "y"), P(rows, "y"))
    return jax.shard_map(local, mesh=fine, in_specs=in_specs, out_specs=out_specs, check_vma=False)
```
